32 devices in a mesh: replica: 1, shard: 8 (over z, x), tensor: 4 (over y, core).
Axes of the slice: x: 2, y: 2, z: 4, core: 2. Of those that a mesh axis runs over, the one named last changes fastest.
Arguments:
- inproj_grads: bfloat16 [1, 1536, 3328], P('replica', 'shard', 'tensor'), may hold values from -6 to 6
- inproj_error: float32 [1, 1536, 3328], P('replica', 'shard', 'tensor'), may hold values from -6 to 6
- inproj_weight: float32 [1536, 3328], P('shard', 'tensor'), may hold values from -6 to 6
- inproj_moment: float32 [1536, 3328], P('shard', 'tensor'), may hold values from -6 to 6
- inproj_query: float32 [3328, 32], P('tensor'), may hold values from -0.109375 to 0.109375
- outproj_grads: bfloat16 [1, 3072, 1536], P('replica', 'shard', 'tensor'), may hold values from -6 to 6
- outproj_error: float32 [1, 3072, 1536], P('replica', 'shard', 'tensor'), may hold values from -6 to 6
- outproj_weight: float32 [3072, 1536], P('shard', 'tensor'), may hold values from -6 to 6
- outproj_moment: float32 [3072, 1536], P('shard', 'tensor'), may hold values from -6 to 6
- outproj_query: float32 [1536, 32], P('tensor'), may hold values from -0.15625 to 0.15625
Outputs:
- inproj_master: float32 [1536, 3328], P('shard', 'tensor')
- inproj_velocity: float32 [1536, 3328], P('shard', 'tensor')
- inproj_residue: float32 [1, 1536, 3328], P('replica', 'shard', 'tensor')
- inproj_basis: float32 [3328, 32], P('tensor')
- outproj_master: float32 [3072, 1536], P('shard', 'tensor')
- outproj_velocity: float32 [3072, 1536], P('shard', 'tensor')
- outproj_residue: float32 [1, 3072, 1536], P('replica', 'shard', 'tensor')
- outproj_basis: float32 [1536, 32], P('tensor')
The draws below stay inside these ranges and needn't reach their ends.
All inputs are finite; a program needn't handle non-finite values.
Results may differ from the reference program's by a relative error of at most 0.0003.
Values sent between devices are 32-bit elements; how exact they have to be, the bound alone decides.
A program may use at most 64 MiB of HBM per device.

```python
import jax
import jax.numpy as jnp
from jax import lax

D = 1536
D_INNER = 3072
RANK = 32
ROUNDS = 2
NS_STEPS = 4
XBC = 3328
N_REPLICA = 1


def shard_levels(rng, shape, pieces, low, high):
    factor_of = 1.0
    for position, shards_of in pieces:
        heights = jax.random.uniform(jax.random.fold_in(jax.random.fold_in(rng, 6), position), (shards_of,), jnp.float32, low / len(pieces), high / len(pieces))
        factor_of = factor_of * jnp.repeat(jnp.exp(heights), shape[position] // shards_of).reshape((-1,) + (1,) * (len(shape) - 1 - position))
    return factor_of


def noise(stream_key, dims, width, limit, shards=(), kind=jnp.bfloat16):
    loudness = shard_levels(stream_key, dims, shards, -0.22, 0.18) if shards else 1.0
    values = jax.random.normal(stream_key, dims, jnp.float32) * width * loudness
    return jnp.minimum(jnp.maximum(values, -limit), limit).astype(kind)


def setup_inputs(seed: int = 0) -> dict:
    splits = jax.random.split(jax.random.key(seed), 11)
    inproj_grads = noise(splits[0], (N_REPLICA, D, XBC), 1.0, 6.0, ((1, 8), (2, 4)))
    inproj_error = noise(splits[1], (N_REPLICA, D, XBC), 0.5, 6.0, ((1, 8), (2, 4)), jnp.float32)
    inproj_weight = noise(splits[2], (D, XBC), 0.5, 6.0, ((0, 8), (1, 4)), jnp.float32)
    inproj_moment = noise(splits[3], (D, XBC), 0.5, 6.0, ((0, 8), (1, 4)), jnp.float32)
    inproj_query = noise(splits[4], (XBC, RANK), XBC ** -0.5, 0.109375, ((0, 4),), jnp.float32)
    outproj_grads = noise(splits[5], (N_REPLICA, D_INNER, D), 1.0, 6.0, ((1, 8), (2, 4)))
    outproj_error = noise(splits[6], (N_REPLICA, D_INNER, D), 0.5, 6.0, ((1, 8), (2, 4)), jnp.float32)
    outproj_weight = noise(splits[7], (D_INNER, D), 0.5, 6.0, ((0, 8), (1, 4)), jnp.float32)
    outproj_moment = noise(splits[8], (D_INNER, D), 0.5, 6.0, ((0, 8), (1, 4)), jnp.float32)
    outproj_query = noise(splits[9], (D, RANK), D ** -0.5, 0.15625, ((0, 4),), jnp.float32)
    return dict(inproj_grads=inproj_grads, inproj_error=inproj_error, inproj_weight=inproj_weight, inproj_moment=inproj_moment, inproj_query=inproj_query, outproj_grads=outproj_grads, outproj_error=outproj_error, outproj_weight=outproj_weight, outproj_moment=outproj_moment, outproj_query=outproj_query)


MOMENTUM_DECAY = 0.9
LEARN_RATE = 0.1
EPSILON = 1e-06

def precise_dot(left, right):
    return jnp.dot(left, right, precision=lax.Precision.HIGHEST, preferred_element_type=jnp.float32)

def inverse_root(gram_sum):
    identity = jnp.eye(gram_sum.shape[0], dtype=jnp.float32)
    norm_scale = jnp.sqrt(jnp.sum(gram_sum * gram_sum) + EPSILON)
    current = gram_sum / norm_scale
    inverse = identity
    for sweep in range(NS_STEPS):
        middle = 0.5 * (3.0 * identity - precise_dot(inverse, current))
        current = precise_dot(current, middle)
        inverse = precise_dot(middle, inverse)
    return inverse / jnp.sqrt(norm_scale)

def compress(grads, error, weight, moment, query):
    merged = grads.astype(jnp.float32) + error
    for power_round in range(ROUNDS):
        projected = jnp.einsum('rnm,mk->nk', merged, query, precision=lax.Precision.HIGHEST) / N_REPLICA
        gram_sum = precise_dot(projected.T, projected)
        orthonormal = precise_dot(projected, inverse_root(gram_sum))
        query = jnp.einsum('rnm,nk->mk', merged, orthonormal, precision=lax.Precision.HIGHEST) / N_REPLICA
    approx = precise_dot(orthonormal, query.T)
    residue = merged - approx[None]
    velocity = MOMENTUM_DECAY * moment + approx
    master = weight - LEARN_RATE * velocity
    return (master, velocity, residue, query)

def reference(inproj_grads, inproj_error, inproj_weight, inproj_moment, inproj_query, outproj_grads, outproj_error, outproj_weight, outproj_moment, outproj_query):
    first = compress(inproj_grads, inproj_error, inproj_weight, inproj_moment, inproj_query)
    second = compress(outproj_grads, outproj_error, outproj_weight, outproj_moment, outproj_query)
    return (first[0], first[1], first[2], first[3], second[0], second[1], second[2], second[3])
```

```python
import functools
import math

import jax
import jax.numpy as jnp
from jax import lax
from jax.experimental import pallas as pl
from jax.experimental.pallas import tpu as pltpu
from jax.sharding import PartitionSpec as P

ROUNDS = 2
NS_STEPS = 4
MOMENTUM_DECAY = 0.9
LEARN_RATE = 0.1
EPSILON = 1e-06
LANES = 128
MESH = pl.DeviceIdType.MESH
F32 = jnp.float32
BF16 = jnp.bfloat16


def up(value, multiple):
    return -(-value // multiple) * multiple


def split(value):
    high = value.astype(BF16)
    low = (value - high.astype(F32)).astype(BF16)
    return high, low


def dot(left, right, contract):
    return lax.dot_general(left, right, ((contract[:1], contract[1:]), ((), ())), preferred_element_type=F32)


def exact(left, right, contract=(1, 0)):
    return lax.dot_general(
        left,
        right,
        ((contract[:1], contract[1:]), ((), ())),
        precision=lax.Precision.HIGHEST,
        preferred_element_type=F32,
    )


def by_matrix(factor, high_ref, low_ref, contract):
    rank = factor.shape[0]
    high, low = split(factor)
    both = dot(jnp.concatenate([high, low], axis=0), high_ref[...], contract)
    return both[:rank] + both[rank:] + dot(high, low_ref[...], contract)


def inverse_roots(grams):
    rank = grams[0].shape[0]
    identity = (
        lax.broadcasted_iota(jnp.int32, (rank, rank), 0) == lax.broadcasted_iota(jnp.int32, (rank, rank), 1)
    ).astype(F32)
    scales = [jnp.sqrt(jnp.sum(gram * gram, keepdims=True) + EPSILON) for gram in grams]
    currents = [gram / scale for gram, scale in zip(grams, scales)]
    inverses = [identity for gram in grams]
    for sweep in range(NS_STEPS):
        products = [current if sweep == 0 else exact(inverse, current) for inverse, current in zip(inverses, currents)]
        middles = [0.5 * (3.0 * identity - product) for product in products]
        inverses = [middle if sweep == 0 else exact(middle, inverse) for middle, inverse in zip(middles, inverses)]
        if sweep < NS_STEPS - 1:
            currents = [exact(current, middle) for current, middle in zip(currents, middles)]
    return [inverse / jnp.sqrt(scale) for inverse, scale in zip(inverses, scales)]


class Group:
    def __init__(self, axes, sizes, rank, width):
        self.axes = axes
        self.sizes = sizes
        self.count = math.prod(sizes)
        down = math.gcd(self.count, max(rank // 8, 1))
        self.across = self.count // down
        self.rows = rank // down
        self.total = up(width, LANES * self.across)
        self.width = self.total // self.across

    def me(self):
        index = 0
        for axis, size in zip(self.axes, self.sizes):
            index = index * size + lax.axis_index(axis)
        return index

    def device(self, index):
        place = {name: lax.axis_index(name) for name in ("replica", "shard", "tensor")}
        for axis, size in reversed(list(zip(self.axes, self.sizes))):
            place[axis] = lax.rem(index, size)
            index = lax.div(index, size)
        return (place["replica"], place["shard"], place["tensor"])

    def peers(self):
        me = self.me()
        return [lax.rem(me + step, self.count) for step in range(1, self.count)]

    def piece(self, index):
        if self.across == 1:
            row, lane = index * self.rows, 0
        else:
            row = lax.div(index, self.across) * self.rows
            lane = pl.multiple_of(lax.rem(index, self.across) * self.width, LANES)
        return (pl.ds(pl.multiple_of(row, 8), self.rows), pl.ds(lane, self.width))

    def slots(self):
        return max(self.count - 1, 1)


def send(group, source, target, sends, receives):
    copies = []
    for step, peer in enumerate(group.peers()):
        copy = pltpu.make_async_remote_copy(
            src_ref=source(peer),
            dst_ref=target(step),
            send_sem=sends.at[step],
            recv_sem=receives.at[step],
            device_id=group.device(peer),
            device_id_type=MESH,
        )
        copy.start()
        copies.append(copy)
    return copies


def factors_kernel(
    left,
    right,
    gram,
    replicas,
    grads_in,
    error_in,
    query_in,
    grads_out,
    error_out,
    query_out,
    ortho_ref,
    stack_ref,
    basis_in,
    basis_out,
    in_high,
    in_low,
    out_high,
    out_low,
    left_part,
    left_slots,
    left_sum,
    right_part,
    right_slots,
    right_sum,
    gram_part,
    gram_slots,
    left_sems,
    right_sems,
    gram_sems,
):
    rank = query_in.shape[0]
    half = rank // 2
    rows_in, cols_in = in_high.shape
    rows_out, cols_out = out_high.shape
    row_at, col_at = up(rows_out, LANES), up(cols_out, LANES)
    barrier = pltpu.get_barrier_semaphore()
    greeted = 0
    for group in (left, right, gram):
        for peer in group.peers():
            pl.semaphore_signal(barrier, inc=1, device_id=group.device(peer), device_id_type=MESH)
            greeted += 1

    merged = grads_in[0].astype(F32) + error_in[0]
    in_high[...], in_low[...] = split(merged)
    merged = grads_out[0].astype(F32) + error_out[0]
    out_high[...], out_low[...] = split(merged)
    left_part[...] = jnp.zeros_like(left_part)
    right_part[...] = jnp.zeros_like(right_part)

    def reduce(group, turn, part, slots, total, sems):
        me = group.me()
        copies = send(group, lambda peer: part.at[turn].at[group.piece(peer)], lambda step: slots.at[turn, step], sems.at[turn, 0], sems.at[turn, 1])
        for copy in copies:
            copy.wait_recv()
        mine = part.at[turn].at[group.piece(me)][...]
        for step in range(group.count - 1):
            mine = mine + slots[turn, step]
        if replicas > 1:
            mine = mine * (1.0 / replicas)
        own = total.at[turn].at[group.piece(me)]
        own[...] = mine
        again = send(group, lambda peer: own, lambda step: own, sems.at[turn, 2], sems.at[turn, 3])
        return copies + again, again

    pending = []
    inverses = None
    for turn in range(ROUNDS):
        if turn == 0:
            factor_in, factor_out = query_in[...], query_out[...]
        left_part[turn, :, :rows_out] = by_matrix(factor_out, out_high, out_low, (1, 1))
        left_part[turn, :, row_at : row_at + rows_in] = by_matrix(factor_in, in_high, in_low, (1, 1))
        if turn == 0:
            pl.semaphore_wait(barrier, greeted)
        copies, gathers = reduce(left, turn, left_part, left_slots, left_sum, left_sems)
        pending += copies
        if turn > 0:
            inverses = gram_roots(gram, turn - 1, gram_part, gram_slots, gram_copies, half)
        for copy in gathers:
            copy.wait_recv()
        projected = left_sum[turn]
        projected_out = projected[:, :rows_out]
        projected_in = projected[:, row_at : row_at + rows_in]
        if turn > 0:
            projected_in = exact(inverses[0], projected_in)
            projected_out = exact(inverses[1], projected_out)
        place = 0
        for value in (projected_in, projected_out):
            product = exact(value, value, (1, 1))
            for start in (0, half):
                gram_part[turn, :, place : place + rank] = product[start : start + half]
                place += rank
        gram_copies = send(
            gram,
            lambda peer: gram_part.at[turn],
            lambda step: gram_slots.at[turn, step],
            gram_sems.at[turn, 0],
            gram_sems.at[turn, 1],
        )
        pending += gram_copies
        right_part[turn, :, :cols_out] = by_matrix(projected_out, out_high, out_low, (1, 0))
        right_part[turn, :, col_at : col_at + cols_in] = by_matrix(projected_in, in_high, in_low, (1, 0))
        copies, gathers = reduce(right, turn, right_part, right_slots, right_sum, right_sems)
        pending += copies
        if turn == ROUNDS - 1:
            inverses = gram_roots(gram, turn, gram_part, gram_slots, gram_copies, half)
            for value, inverse, start, size in (
                (projected_out, inverses[1], 0, rows_out),
                (projected_in, inverses[0], row_at, rows_in),
            ):
                high, low = split(exact(inverse, value))
                tall = jnp.concatenate([high, high, low], axis=0).astype(F32)
                ortho_ref[start : start + size, :] = jnp.transpose(tall).astype(BF16)
        for copy in gathers:
            copy.wait_recv()
        factor_out = right_sum[turn, :, :cols_out]
        factor_in = right_sum[turn, :, col_at : col_at + cols_in]
    basis_in[...] = exact(inverses[0], factor_in)
    basis_out[...] = exact(inverses[1], factor_out)
    for value, start, size in ((basis_out, 0, cols_out), (basis_in, col_at, cols_in)):
        high, low = split(value[...])
        stack_ref[:, start : start + size] = jnp.concatenate([high, low, high], axis=0)
    for copy in pending:
        copy.wait_send()


def gram_roots(gram, turn, part, slots, copies, half):
    for copy in copies:
        copy.wait_recv()
    total = part[turn]
    for step in range(gram.count - 1):
        total = total + slots[turn, step]
    rank = 2 * half
    grams = []
    for place in (0, 2 * rank):
        grams.append(
            jnp.concatenate([total[:, place : place + rank], total[:, place + rank : place + 2 * rank]], axis=0)
        )
    return inverse_roots(grams)


def finish_kernel(
    offsets,
    steps,
    grads_in,
    error_in,
    weight_in,
    moment_in,
    grads_out,
    error_out,
    weight_out,
    moment_out,
    ortho_ref,
    stack_ref,
    master_in,
    velocity_in,
    residue_in,
    master_out,
    velocity_out,
    residue_out,
):
    row_at, col_at = offsets
    step = pl.program_id(0)
    for grads, error, weight, moment, master, velocity, residue, row, col in (
        (grads_in, error_in, weight_in, moment_in, master_in, velocity_in, residue_in, row_at, col_at),
        (grads_out, error_out, weight_out, moment_out, master_out, velocity_out, residue_out, 0, 0),
    ):
        rows, cols = weight.shape
        left = ortho_ref[pl.ds(pl.multiple_of(row + step * rows, 16), rows), :]
        approx = dot(left, stack_ref[:, col : col + cols], (1, 0))
        residue[0] = grads[0].astype(F32) + error[0] - approx
        speed = MOMENTUM_DECAY * moment[...] + approx
        velocity[...] = speed
        master[...] = weight[...] - LEARN_RATE * speed


def per_device(sizes, *arrays):
    grads_in, error_in, weight_in, moment_in, query_in = arrays[:5]
    grads_out, error_out, weight_out, moment_out, query_out = arrays[5:]
    replicas, shards, tensors = sizes
    rows_in, cols_in = weight_in.shape
    rows_out, cols_out = weight_out.shape
    rank = query_in.shape[1]
    row_at, col_at = up(rows_out, LANES), up(cols_out, LANES)
    left = Group(("replica", "tensor"), (replicas, tensors), rank, row_at + rows_in)
    right = Group(("replica", "shard"), (replicas, shards), rank, col_at + cols_in)
    gram = Group(("shard",), (shards,), rank, LANES)
    vmem = pl.BlockSpec(memory_space=pltpu.VMEM)
    packed = up(4 * rank, LANES)

    def room(group):
        return [
            pltpu.VMEM((ROUNDS, rank, group.total), F32),
            pltpu.VMEM((ROUNDS, group.slots(), group.rows, group.width), F32),
            pltpu.VMEM((ROUNDS, rank, group.total), F32),
        ]

    ortho, stack, basis_in, basis_out = pl.pallas_call(
        functools.partial(factors_kernel, left, right, gram, replicas),
        out_shape=(
            jax.ShapeDtypeStruct((row_at + up(rows_in, LANES), 3 * rank), BF16),
            jax.ShapeDtypeStruct((3 * rank, col_at + up(cols_in, LANES)), BF16),
            jax.ShapeDtypeStruct((rank, cols_in), F32),
            jax.ShapeDtypeStruct((rank, cols_out), F32),
        ),
        in_specs=[vmem] * 6,
        out_specs=(vmem,) * 4,
        scratch_shapes=[
            pltpu.VMEM((rows_in, cols_in), BF16),
            pltpu.VMEM((rows_in, cols_in), BF16),
            pltpu.VMEM((rows_out, cols_out), BF16),
            pltpu.VMEM((rows_out, cols_out), BF16),
            *room(left),
            *room(right),
            pltpu.VMEM((ROUNDS, rank // 2, packed), F32),
            pltpu.VMEM((ROUNDS, gram.slots(), rank // 2, packed), F32),
            pltpu.SemaphoreType.DMA((ROUNDS, 4, left.slots())),
            pltpu.SemaphoreType.DMA((ROUNDS, 4, right.slots())),
            pltpu.SemaphoreType.DMA((ROUNDS, 2, gram.slots())),
        ],
        compiler_params=pltpu.CompilerParams(collective_id=0, has_side_effects=True, vmem_limit_bytes=24 << 20),
        name="factors",
    )(grads_in, error_in, query_in.T, grads_out, error_out, query_out.T)

    steps = math.gcd(rows_in // 16, rows_out // 16, 4)

    def block(array):
        if array.ndim == 3:
            return pl.BlockSpec((1, array.shape[1] // steps, array.shape[2]), lambda step: (0, step, 0))
        return pl.BlockSpec((array.shape[0] // steps, array.shape[1]), lambda step: (step, 0))

    operands = (grads_in, error_in, weight_in, moment_in, grads_out, error_out, weight_out, moment_out)
    results = (weight_in, moment_in, error_in, weight_out, moment_out, error_out)
    finished = pl.pallas_call(
        functools.partial(finish_kernel, (row_at, col_at), steps),
        grid=(steps,),
        out_shape=tuple(jax.ShapeDtypeStruct(array.shape, F32) for array in results),
        in_specs=[block(array) for array in operands] + [vmem, vmem],
        out_specs=tuple(block(array) for array in results),
        compiler_params=pltpu.CompilerParams(vmem_limit_bytes=24 << 20),
        name="finish",
    )(*operands, ortho, stack)
    return (*finished[:3], basis_in.T, *finished[3:], basis_out.T)


def solution(mesh):
    sizes = (mesh.shape["replica"], mesh.shape["shard"], mesh.shape["tensor"])
    cube, flat, thin = P("replica", "shard", "tensor"), P("shard", "tensor"), P("tensor", None)
    return jax.shard_map(
        functools.partial(per_device, sizes),
        mesh=mesh,
        in_specs=(cube, cube, flat, flat, thin) * 2,
        out_specs=(flat, flat, cube, thin) * 2,
        check_vma=False,
    )
```

```python
import functools
import math

import jax
import jax.numpy as jnp
from jax import lax
from jax.experimental import pallas as pl
from jax.experimental.pallas import tpu as pltpu
from jax.sharding import PartitionSpec as P

ROUNDS = 2
NS_STEPS = 4
MOMENTUM_DECAY = 0.9
LEARN_RATE = 0.1
EPSILON = 1e-06
LANES = 128
MESH = pl.DeviceIdType.MESH
F32 = jnp.float32
BF16 = jnp.bfloat16


def up(value, multiple):
    return -(-value // multiple) * multiple


def split(value):
    high = value.astype(BF16)
    low = (value - high.astype(F32)).astype(BF16)
    return high, low


def dot(left, right, contract):
    return lax.dot_general(left, right, ((contract[:1], contract[1:]), ((), ())), preferred_element_type=F32)


def exact(left, right, contract=(1, 0)):
    return lax.dot_general(
        left,
        right,
        ((contract[:1], contract[1:]), ((), ())),
        precision=lax.Precision.HIGHEST,
        preferred_element_type=F32,
    )


def by_matrix(factor, high_ref, low_ref, contract):
    rank = factor.shape[0]
    high, low = split(factor)
    both = dot(jnp.concatenate([high, low], axis=0), high_ref[...], contract)
    return both[:rank] + both[rank:] + dot(high, low_ref[...], contract)


def inverse_roots(grams):
    rank = grams[0].shape[0]
    identity = (
        lax.broadcasted_iota(jnp.int32, (rank, rank), 0) == lax.broadcasted_iota(jnp.int32, (rank, rank), 1)
    ).astype(F32)
    scales = [jnp.sqrt(jnp.sum(gram * gram, keepdims=True) + EPSILON) for gram in grams]
    currents = [gram / scale for gram, scale in zip(grams, scales)]
    inverses = [identity for gram in grams]
    for sweep in range(NS_STEPS):
        products = [current if sweep == 0 else exact(inverse, current) for inverse, current in zip(inverses, currents)]
        middles = [0.5 * (3.0 * identity - product) for product in products]
        inverses = [middle if sweep == 0 else exact(middle, inverse) for middle, inverse in zip(middles, inverses)]
        if sweep < NS_STEPS - 1:
            currents = [exact(current, middle) for current, middle in zip(currents, middles)]
    return [inverse / jnp.sqrt(scale) for inverse, scale in zip(inverses, scales)]


class Group:
    def __init__(self, axes, sizes, rank, width):
        self.axes = axes
        self.sizes = sizes
        self.count = math.prod(sizes)
        self.down = math.gcd(self.count, max(rank // 8, 1))
        self.across = self.count // self.down
        self.rows = rank // self.down
        self.total = up(width, LANES * self.across)
        self.width = self.total // self.across

    def index(self):
        index = 0
        for axis, size in zip(self.axes, self.sizes):
            index = index * size + lax.axis_index(axis)
        return index

    def place(self):
        index = self.index()
        return lax.div(index, self.across), lax.rem(index, self.across)

    def device(self, down, across):
        index = down * self.across + across
        place = {name: lax.axis_index(name) for name in ("replica", "shard", "tensor")}
        for axis, size in reversed(list(zip(self.axes, self.sizes))):
            place[axis] = lax.rem(index, size)
            index = lax.div(index, size)
        return (place["replica"], place["shard"], place["tensor"])

    def near(self):
        down, across = self.place()
        return [
            ((self.down - 1) * self.across + step - 1, down, lax.rem(across + step, self.across))
            for step in range(1, self.across)
        ]

    def far(self, across):
        down, mine = self.place()
        return [
            ((step - 1) * self.across + mine, lax.rem(down + step, self.down), across) for step in range(1, self.down)
        ]

    def peers(self):
        return [peer for part in range(self.across) for peer in self.far(part)] + self.near()

    def near_slots(self):
        return [(self.down - 1) * self.across + step - 1 for step in range(1, self.across)]

    def far_slots(self, across):
        return [(step - 1) * self.across + across for step in range(1, self.down)]

    def all_slots(self):
        return range(self.count - 1)

    def piece(self, down, across):
        row = pl.multiple_of(down * self.rows, 8)
        lane = 0 if self.across == 1 else pl.multiple_of(across * self.width, LANES)
        return (pl.ds(row, self.rows), pl.ds(lane, self.width))

    def slots(self):
        return max(self.count - 1, 1)


class Exchange:
    def __init__(self, group, replicas, part, slots, total, sems):
        self.group, self.replicas = group, replicas
        self.part, self.slots, self.total, self.sems = part, slots, total, sems
        self.started = []

    def copy(self, source, target, stage, slot, peer):
        return pltpu.make_async_remote_copy(
            src_ref=source,
            dst_ref=target,
            send_sem=self.sems.at[stage, slot],
            recv_sem=self.sems.at[stage + 1, slot],
            device_id=self.group.device(*peer),
            device_id_type=MESH,
        )

    def start(self, copy):
        copy.start()
        self.started.append(copy)

    def scatter(self, peers):
        for slot, *peer in peers:
            self.start(self.copy(self.part.at[self.group.piece(*peer)], self.slots.at[slot], 0, slot, peer))

    def arrive(self, stage, slots, target):
        place = self.group.place()
        for slot in slots:
            target_ref = target(slot)
            self.copy(target_ref, target_ref, stage, slot, place).wait_recv()

    def gather(self):
        group = self.group
        self.arrive(0, group.all_slots(), lambda slot: self.slots.at[slot])
        piece = group.piece(*group.place())
        mine = self.part.at[piece][...]
        for slot in group.all_slots():
            mine = mine + self.slots[slot]
        if self.replicas > 1:
            mine = mine * (1.0 / self.replicas)
        own = self.total.at[piece]
        own[...] = mine
        for slot, *peer in group.peers():
            self.start(self.copy(own, own, 2, slot, peer))

    def finish(self, slots):
        own = self.total.at[self.group.piece(*self.group.place())]
        self.arrive(2, slots, lambda slot: own)

    def broadcast(self):
        for slot, *peer in self.group.peers():
            self.start(self.copy(self.part, self.slots.at[slot], 0, slot, peer))

    def collect(self):
        self.arrive(0, self.group.all_slots(), lambda slot: self.slots.at[slot])
        total = self.part[...]
        for slot in self.group.all_slots():
            total = total + self.slots[slot]
        return total


def factors_kernel(groups, replicas, *refs):
    left_out, left_in, right, gram = groups
    sources, refs = refs[:10], refs[10:]
    merged, weights, moments, refs = refs[:2], refs[2:4], refs[4:6], refs[6:]
    ortho_ref, stack_ref, bases, refs = refs[0], refs[1], refs[2:4], refs[4:]
    grads, errors, queries, refs = refs[:2], refs[2:4], refs[4:6], refs[6:]
    highs, lows, refs = refs[:2], refs[2:4], refs[4:]
    load_sems, rooms = refs[0], [refs[1 + 4 * place : 5 + 4 * place] for place in range(4)]
    rank = queries[0].shape[0]
    half = rank // 2
    (rows_in, cols_in), (rows_out, cols_out) = merged[0].shape, merged[1].shape
    row_at, col_at = up(rows_out, LANES), up(cols_out, LANES)
    gram_at = col_at + cols_in
    targets = (
        grads[0], errors[0], weights[0], moments[0], queries[0],
        grads[1], errors[1], weights[1], moments[1], queries[1],
    )
    loads = [
        pltpu.make_async_copy(source, target, load_sems.at[place])
        for place, (source, target) in enumerate(zip(sources, targets))
    ]
    for place in (6, 5, 9, 1, 0, 4, 2, 3, 7, 8):
        loads[place].start()

    barrier = pltpu.get_barrier_semaphore()
    greeted = 0
    for group in groups:
        for slot, *peer in group.peers():
            pl.semaphore_signal(barrier, inc=1, device_id=group.device(*peer), device_id_type=MESH)
            greeted += 1

    for part in (rooms[0][0], rooms[1][0], rooms[2][0]):
        part[...] = jnp.zeros_like(part)
    exchanges = [
        [
            Exchange(group, count, part.at[turn], slots.at[turn], total.at[turn], sems.at[turn])
            for group, count, (part, slots, total, sems) in zip(groups, (replicas, replicas, replicas, 1), rooms)
        ]
        for turn in range(ROUNDS)
    ]

    def merge(which, first):
        for place in (first, first + 1, first + 4):
            loads[place].wait()
        value = grads[which][0].astype(F32) + errors[which][0]
        merged[which][...] = value
        highs[which][...], lows[which][...] = split(value)

    inverses = None
    for turn in range(ROUNDS):
        sum_out, sum_in, sum_right, sum_gram = exchanges[turn]
        if turn == 0:
            merge(1, 5)
            factor_out = queries[1][...]
        else:
            before = exchanges[turn - 1][2]
            before.finish(right.near_slots())
            waited = 0
            while waited * right.width < cols_out:
                before.finish(right.far_slots(waited))
                waited += 1
            factor_out = before.total[:, :cols_out]
        sum_out.part[:, :rows_out] = by_matrix(factor_out, highs[1], lows[1], (1, 1))
        if turn == 0:
            pl.semaphore_wait(barrier, greeted)
        sum_out.scatter(sum_out.group.peers())
        if turn == 0:
            merge(0, 0)
            factor_in = queries[0][...]
        else:
            for part in range(waited, right.across):
                before.finish(right.far_slots(part))
            factor_in = before.total[:, col_at : col_at + cols_in]
        sum_in.part[:, :rows_in] = by_matrix(factor_in, highs[0], lows[0], (1, 1))
        sum_in.scatter(sum_in.group.peers())
        sum_out.gather()
        sum_in.gather()
        if turn > 0:
            grams = before.total[:, gram_at : gram_at + 2 * rank]
            inverses = inverse_roots((grams[:, :rank], grams[:, rank:]))
        sum_out.finish(left_out.all_slots())
        projected_out = sum_out.total[:, :rows_out]
        if turn > 0:
            projected_out = exact(inverses[1], projected_out)
        sum_right.part[:, :cols_out] = by_matrix(projected_out, highs[1], lows[1], (1, 0))
        sum_in.finish(left_in.all_slots())
        projected_in = sum_in.total[:, :rows_in]
        if turn > 0:
            projected_in = exact(inverses[0], projected_in)
        products = [exact(value, value, (1, 1)) for value in (projected_in, projected_out)]
        if turn < ROUNDS - 1:
            for place, product in enumerate(products):
                start = gram_at + place * rank
                sum_right.part[:, start : start + rank] = product
        else:
            for place, product in enumerate(products):
                for step in range(2):
                    start = (2 * place + step) * rank
                    sum_gram.part[:, start : start + rank] = product[step * half : step * half + half]
            sum_gram.broadcast()
        done = col_at
        for part in range(right.across):
            stop = min((part + 1) * right.width, gram_at)
            if stop > done:
                columns = (slice(None), slice(done - col_at, stop - col_at))
                sum_right.part[:, done:stop] = by_matrix(projected_in, highs[0].at[columns], lows[0].at[columns], (1, 0))
                done = stop
            sum_right.scatter(right.far(part))
        sum_right.scatter(right.near())
        sum_right.gather()
    for place in (2, 3, 7, 8):
        loads[place].wait()
    total = sum_gram.collect()
    grams = [
        jnp.concatenate([total[:, place : place + rank], total[:, place + rank : place + 2 * rank]], axis=0)
        for place in (0, 2 * rank)
    ]
    inverses = inverse_roots(grams)
    for value, inverse, start, size in (
        (projected_out, inverses[1], 0, rows_out),
        (projected_in, inverses[0], row_at, rows_in),
    ):
        high, low = split(exact(inverse, value))
        tall = jnp.concatenate([high, high, low], axis=0).astype(F32)
        ortho_ref[start : start + size, :] = jnp.transpose(tall).astype(BF16)
    sum_right.finish(right.all_slots())
    for which, start, size in ((1, 0, cols_out), (0, col_at, cols_in)):
        value = exact(inverses[which], sum_right.total[:, start : start + size])
        bases[which][...] = value
        high, low = split(value)
        stack_ref[:, start : start + size] = jnp.concatenate([high, low, high], axis=0)
    for turn in exchanges:
        for exchange in turn:
            for copy in exchange.started:
                copy.wait_send()


def finish_kernel(offsets, *refs):
    merged, weights, moments, refs = refs[:2], refs[2:4], refs[4:6], refs[6:]
    ortho_ref, stack_ref, bases, refs = refs[0], refs[1], refs[2:4], refs[4:]
    outputs = (refs[:4], refs[4:])
    step = pl.program_id(0)

    @pl.when(step == 0)
    def _():
        for basis, output in zip(bases, outputs):
            output[3][...] = basis[...]

    for which, (row, col) in enumerate((offsets, (0, 0))):
        master, velocity, residue = outputs[which][:3]
        rows, cols = master.shape
        here = pl.ds(pl.multiple_of(step * rows, 16), rows)
        left = ortho_ref[pl.ds(pl.multiple_of(row + step * rows, 16), rows), :]
        approx = dot(left, stack_ref[:, col : col + cols], (1, 0))
        residue[0] = merged[which][here, :] - approx
        speed = MOMENTUM_DECAY * moments[which][here, :] + approx
        velocity[...] = speed
        master[...] = weights[which][here, :] - LEARN_RATE * speed


def per_device(sizes, *arrays):
    weight_in, weight_out, query_in = arrays[2], arrays[7], arrays[4]
    replicas, shards, tensors = sizes
    rows_in, cols_in = weight_in.shape
    rows_out, cols_out = weight_out.shape
    rank = query_in.shape[1]
    row_at, col_at = up(rows_out, LANES), up(cols_out, LANES)
    left_axes = (("replica", "tensor"), (replicas, tensors), rank)
    left_out, left_in = Group(*left_axes, rows_out), Group(*left_axes, rows_in)
    right = Group(("replica", "shard"), (replicas, shards), rank, col_at + cols_in + 2 * rank)
    gram = Group(("shard",), (shards,), rank, LANES)
    groups = (left_out, left_in, right, gram)
    vmem = pl.BlockSpec(memory_space=pltpu.VMEM)
    packed = up(4 * rank, LANES)

    def room(group):
        return [
            pltpu.VMEM((ROUNDS, rank, group.total), F32),
            pltpu.VMEM((ROUNDS, group.slots(), group.rows, group.width), F32),
            pltpu.VMEM((ROUNDS, rank, group.total), F32),
            pltpu.SemaphoreType.DMA((ROUNDS, 4, group.slots())),
        ]

    both = (weight_in.shape, weight_out.shape)
    operands = [array.T if array.shape[-1] == rank else array for array in arrays]
    operands = [pltpu.with_memory_space_constraint(array, pltpu.HBM) for array in operands]
    carried = pl.pallas_call(
        functools.partial(factors_kernel, groups, replicas),
        out_shape=(
            *[jax.ShapeDtypeStruct(shape, F32) for shape in both * 3],
            jax.ShapeDtypeStruct((row_at + up(rows_in, LANES), 3 * rank), BF16),
            jax.ShapeDtypeStruct((3 * rank, col_at + up(cols_in, LANES)), BF16),
            jax.ShapeDtypeStruct((rank, cols_in), F32),
            jax.ShapeDtypeStruct((rank, cols_out), F32),
        ),
        in_specs=[pl.BlockSpec(memory_space=pltpu.HBM)] * 10,
        out_specs=(vmem,) * 10,
        scratch_shapes=[
            *[pltpu.VMEM((1, *shape), BF16) for shape in both],
            *[pltpu.VMEM((1, *shape), F32) for shape in both],
            *[pltpu.VMEM((rank, shape[1]), F32) for shape in both],
            *[pltpu.VMEM(shape, BF16) for shape in both * 2],
            pltpu.SemaphoreType.DMA((10,)),
            *[space for group in groups[:3] for space in room(group)],
            pltpu.VMEM((ROUNDS, rank // 2, packed), F32),
            pltpu.VMEM((ROUNDS, gram.slots(), rank // 2, packed), F32),
            pltpu.VMEM((ROUNDS, 8, packed), F32),
            pltpu.SemaphoreType.DMA((ROUNDS, 2, gram.slots())),
        ],
        compiler_params=pltpu.CompilerParams(collective_id=0, has_side_effects=True, vmem_limit_bytes=24 << 20),
        name="factors",
    )(*operands)

    steps = math.gcd(rows_in // 16, rows_out // 16, 4)

    def rows_of(shape):
        return pl.BlockSpec((shape[0] // steps, shape[1]), lambda step: (step, 0))

    def cube_of(shape):
        return pl.BlockSpec((1, shape[0] // steps, shape[1]), lambda step: (0, step, 0))

    results, specs = [], []
    for shape in both:
        results += [shape, shape, (1, *shape), (rank, shape[1])]
        specs += [rows_of(shape), rows_of(shape), cube_of(shape), pl.BlockSpec((rank, shape[1]), lambda step: (0, 0))]
    finished = pl.pallas_call(
        functools.partial(finish_kernel, (row_at, col_at)),
        grid=(steps,),
        out_shape=tuple(jax.ShapeDtypeStruct(shape, F32) for shape in results),
        in_specs=[vmem] * 10,
        out_specs=tuple(specs),
        compiler_params=pltpu.CompilerParams(vmem_limit_bytes=24 << 20),
        name="finish",
    )(*carried)
    return tuple(array.T if place % 4 == 3 else array for place, array in enumerate(finished))


def solution(mesh):
    sizes = (mesh.shape["replica"], mesh.shape["shard"], mesh.shape["tensor"])
    cube, flat, thin = P("replica", "shard", "tensor"), P("shard", "tensor"), P("tensor", None)
    return jax.shard_map(
        functools.partial(per_device, sizes),
        mesh=mesh,
        in_specs=(cube, cube, flat, flat, thin) * 2,
        out_specs=(flat, flat, cube, thin) * 2,
        check_vma=False,
    )
```

```python
import functools
import math

import jax
import jax.numpy as jnp
from jax import lax
from jax.experimental import pallas as pl
from jax.experimental.pallas import tpu as pltpu
from jax.sharding import PartitionSpec as P

ROUNDS = 2
NS_STEPS = 4
MOMENTUM_DECAY = 0.9
LEARN_RATE = 0.1
EPSILON = 1e-06
LANES = 128
MESH = pl.DeviceIdType.MESH
F32 = jnp.float32
BF16 = jnp.bfloat16


def up(value, multiple):
    return -(-value // multiple) * multiple


def split(value):
    high = value.astype(BF16)
    low = (value - high.astype(F32)).astype(BF16)
    return high, low


def dot(left, right, contract):
    return lax.dot_general(left, right, ((contract[:1], contract[1:]), ((), ())), preferred_element_type=F32)


def by_parts(factor, parts, contract):
    rank = factor.shape[0]
    high, low = split(factor)
    both = dot(jnp.concatenate([high, low], axis=0), parts[0], contract)
    return both[:rank] + both[rank:] + dot(high, parts[1], contract)


def by_matrix(factor, high_ref, low_ref, contract):
    return by_parts(factor, (high_ref[...], low_ref[...]), contract)


def product_of(left, right, contract=(1, 0)):
    return by_parts(left, split(right), contract)


def inverse_roots(grams):
    rank = grams[0].shape[0]
    identity = (
        lax.broadcasted_iota(jnp.int32, (rank, rank), 0) == lax.broadcasted_iota(jnp.int32, (rank, rank), 1)
    ).astype(F32)
    scales = [jnp.sqrt(jnp.sum(gram * gram, keepdims=True) + EPSILON) for gram in grams]
    currents = [gram / scale for gram, scale in zip(grams, scales)]
    inverses = [identity for gram in grams]
    for sweep in range(NS_STEPS):
        products = [current if sweep == 0 else product_of(inverse, current) for inverse, current in zip(inverses, currents)]
        middles = [0.5 * (3.0 * identity - product) for product in products]
        inverses = [middle if sweep == 0 else product_of(middle, inverse) for middle, inverse in zip(middles, inverses)]
        if sweep < NS_STEPS - 1:
            currents = [product_of(current, middle) for current, middle in zip(currents, middles)]
    return [inverse / jnp.sqrt(scale) for inverse, scale in zip(inverses, scales)]


class Group:
    def __init__(self, axes, sizes, rank, width):
        self.axes = axes
        self.sizes = sizes
        self.count = math.prod(sizes)
        self.down = math.gcd(self.count, max(rank // 8, 1))
        self.across = self.count // self.down
        self.rows = rank // self.down
        self.total = up(width, LANES * self.across)
        self.width = self.total // self.across

    def index(self):
        index = 0
        for axis, size in zip(self.axes, self.sizes):
            index = index * size + lax.axis_index(axis)
        return index

    def place(self):
        index = self.index()
        return lax.div(index, self.across), lax.rem(index, self.across)

    def device(self, down, across):
        index = down * self.across + across
        place = {name: lax.axis_index(name) for name in ("replica", "shard", "tensor")}
        for axis, size in reversed(list(zip(self.axes, self.sizes))):
            place[axis] = lax.rem(index, size)
            index = lax.div(index, size)
        return (place["replica"], place["shard"], place["tensor"])

    def near(self):
        down, across = self.place()
        return [
            ((self.down - 1) * self.across + step - 1, down, lax.rem(across + step, self.across))
            for step in range(1, self.across)
        ]

    def far(self, across):
        down, mine = self.place()
        return [
            ((step - 1) * self.across + mine, lax.rem(down + step, self.down), across) for step in range(1, self.down)
        ]

    def peers(self):
        return [peer for part in range(self.across) for peer in self.far(part)] + self.near()

    def near_slots(self):
        return [(self.down - 1) * self.across + step - 1 for step in range(1, self.across)]

    def far_slots(self, across):
        return [(step - 1) * self.across + across for step in range(1, self.down)]

    def all_slots(self):
        return range(self.count - 1)

    def piece(self, down, across):
        row = pl.multiple_of(down * self.rows, 8)
        lane = 0 if self.across == 1 else pl.multiple_of(across * self.width, LANES)
        return (pl.ds(row, self.rows), pl.ds(lane, self.width))

    def slots(self):
        return max(self.count - 1, 1)


class Exchange:
    def __init__(self, group, replicas, part, slots, total, sems):
        self.group, self.replicas = group, replicas
        self.part, self.slots, self.total, self.sems = part, slots, total, sems
        self.started = []

    def copy(self, source, target, stage, slot, peer):
        return pltpu.make_async_remote_copy(
            src_ref=source,
            dst_ref=target,
            send_sem=self.sems.at[stage, slot],
            recv_sem=self.sems.at[stage + 1, slot],
            device_id=self.group.device(*peer),
            device_id_type=MESH,
        )

    def start(self, copy):
        copy.start()
        self.started.append(copy)

    def scatter(self, peers):
        for slot, *peer in peers:
            self.start(self.copy(self.part.at[self.group.piece(*peer)], self.slots.at[slot], 0, slot, peer))

    def arrive(self, stage, slots, target):
        place = self.group.place()
        for slot in slots:
            target_ref = target(slot)
            self.copy(target_ref, target_ref, stage, slot, place).wait_recv()

    def gather(self):
        group = self.group
        self.arrive(0, group.all_slots(), lambda slot: self.slots.at[slot])
        piece = group.piece(*group.place())
        mine = self.part.at[piece][...]
        for slot in group.all_slots():
            mine = mine + self.slots[slot]
        if self.replicas > 1:
            mine = mine * (1.0 / self.replicas)
        own = self.total.at[piece]
        own[...] = mine
        for slot, *peer in group.peers():
            self.start(self.copy(own, own, 2, slot, peer))

    def finish(self, slots):
        own = self.total.at[self.group.piece(*self.group.place())]
        self.arrive(2, slots, lambda slot: own)

    def broadcast(self):
        for slot, *peer in self.group.peers():
            self.start(self.copy(self.part, self.slots.at[slot], 0, slot, peer))

    def collect(self):
        self.arrive(0, self.group.all_slots(), lambda slot: self.slots.at[slot])
        total = self.part[...]
        for slot in self.group.all_slots():
            total = total + self.slots[slot]
        return total


def factors_kernel(groups, replicas, *refs):
    left_out, left_in, right, gram = groups
    sources, refs = refs[:10], refs[10:]
    merged, weights, moments, refs = refs[:2], refs[2:4], refs[4:6], refs[6:]
    ortho_ref, stack_ref, bases, refs = refs[0], refs[1], refs[2:4], refs[4:]
    grads, errors, queries, refs = refs[:2], refs[2:4], refs[4:6], refs[6:]
    highs, lows, refs = refs[:2], refs[2:4], refs[4:]
    load_sems, rooms = refs[0], [refs[1 + 4 * place : 5 + 4 * place] for place in range(4)]
    rank = queries[0].shape[0]
    half = rank // 2
    (rows_in, cols_in), (rows_out, cols_out) = merged[0].shape, merged[1].shape
    row_at, col_at = up(rows_out, LANES), up(cols_out, LANES)
    gram_at = col_at + cols_in
    targets = (
        grads[0], errors[0], weights[0], moments[0], queries[0],
        grads[1], errors[1], weights[1], moments[1], queries[1],
    )
    loads = [
        pltpu.make_async_copy(source, target, load_sems.at[place])
        for place, (source, target) in enumerate(zip(sources, targets))
    ]
    for place in (6, 5, 9, 1, 0, 4, 2, 3, 7, 8):
        loads[place].start()

    barrier = pltpu.get_barrier_semaphore()
    greeted = 0
    for group in groups:
        for slot, *peer in group.peers():
            pl.semaphore_signal(barrier, inc=1, device_id=group.device(*peer), device_id_type=MESH)
            greeted += 1

    for part in (rooms[0][0], rooms[1][0], rooms[2][0]):
        part[...] = jnp.zeros_like(part)
    exchanges = [
        [
            Exchange(group, count, part.at[turn], slots.at[turn], total.at[turn], sems.at[turn])
            for group, count, (part, slots, total, sems) in zip(groups, (replicas, replicas, replicas, 1), rooms)
        ]
        for turn in range(ROUNDS)
    ]

    def merge(which, first):
        for place in (first, first + 1, first + 4):
            loads[place].wait()
        value = grads[which][0].astype(F32) + errors[which][0]
        merged[which][...] = value
        highs[which][...], lows[which][...] = split(value)

    inverses = None
    for turn in range(ROUNDS):
        sum_out, sum_in, sum_right, sum_gram = exchanges[turn]
        if turn == 0:
            merge(1, 5)
            factor_out = queries[1][...]
        else:
            before = exchanges[turn - 1][2]
            before.finish(right.near_slots())
            waited = 0
            while waited * right.width < cols_out:
                before.finish(right.far_slots(waited))
                waited += 1
            factor_out = before.total[:, :cols_out]
        sum_out.part[:, :rows_out] = by_matrix(factor_out, highs[1], lows[1], (1, 1))
        if turn == 0:
            pl.semaphore_wait(barrier, greeted)
        sum_out.scatter(sum_out.group.peers())
        if turn == 0:
            merge(0, 0)
            factor_in = queries[0][...]
        else:
            for part in range(waited, right.across):
                before.finish(right.far_slots(part))
            factor_in = before.total[:, col_at : col_at + cols_in]
        sum_in.part[:, :rows_in] = by_matrix(factor_in, highs[0], lows[0], (1, 1))
        sum_in.scatter(sum_in.group.peers())
        sum_out.gather()
        sum_in.gather()
        if turn > 0:
            grams = before.total[:, gram_at : gram_at + 2 * rank]
            inverses = inverse_roots((grams[:, :rank], grams[:, rank:]))
        sum_out.finish(left_out.all_slots())
        projected_out = sum_out.total[:, :rows_out]
        if turn > 0:
            projected_out = product_of(inverses[1], projected_out)
        sum_right.part[:, :cols_out] = by_matrix(projected_out, highs[1], lows[1], (1, 0))
        sum_in.finish(left_in.all_slots())
        projected_in = sum_in.total[:, :rows_in]
        if turn > 0:
            projected_in = product_of(inverses[0], projected_in)
        products = [product_of(value, value, (1, 1)) for value in (projected_in, projected_out)]
        if turn < ROUNDS - 1:
            for place, product in enumerate(products):
                start = gram_at + place * rank
                sum_right.part[:, start : start + rank] = product
        else:
            for place, product in enumerate(products):
                for step in range(2):
                    start = (2 * place + step) * rank
                    sum_gram.part[:, start : start + rank] = product[step * half : step * half + half]
            sum_gram.broadcast()
        done = col_at
        for part in range(right.across):
            stop = min((part + 1) * right.width, gram_at)
            if stop > done:
                columns = (slice(None), slice(done - col_at, stop - col_at))
                sum_right.part[:, done:stop] = by_matrix(projected_in, highs[0].at[columns], lows[0].at[columns], (1, 0))
                done = stop
            sum_right.scatter(right.far(part))
        sum_right.scatter(right.near())
        sum_right.gather()
    for place in (2, 3, 7, 8):
        loads[place].wait()
    total = sum_gram.collect()
    grams = [
        jnp.concatenate([total[:, place : place + rank], total[:, place + rank : place + 2 * rank]], axis=0)
        for place in (0, 2 * rank)
    ]
    inverses = inverse_roots(grams)
    for value, inverse, start, size in (
        (projected_out, inverses[1], 0, rows_out),
        (projected_in, inverses[0], row_at, rows_in),
    ):
        high, low = split(product_of(inverse, value))
        tall = jnp.concatenate([high, high, low], axis=0).astype(F32)
        ortho_ref[start : start + size, :] = jnp.transpose(tall).astype(BF16)
    sum_right.finish(right.all_slots())
    for which, start, size in ((1, 0, cols_out), (0, col_at, cols_in)):
        value = product_of(inverses[which], sum_right.total[:, start : start + size])
        bases[which][...] = value
        high, low = split(value)
        stack_ref[:, start : start + size] = jnp.concatenate([high, low, high], axis=0)
    for turn in exchanges:
        for exchange in turn:
            for copy in exchange.started:
                copy.wait_send()


def finish_kernel(offsets, *refs):
    merged, weights, moments, refs = refs[:2], refs[2:4], refs[4:6], refs[6:]
    ortho_ref, stack_ref, bases, refs = refs[0], refs[1], refs[2:4], refs[4:]
    outputs = (refs[:4], refs[4:])
    step = pl.program_id(0)

    @pl.when(step == 0)
    def _():
        for basis, output in zip(bases, outputs):
            output[3][...] = basis[...]

    for which, (row, col) in enumerate((offsets, (0, 0))):
        master, velocity, residue = outputs[which][:3]
        rows, cols = master.shape
        here = pl.ds(pl.multiple_of(step * rows, 16), rows)
        left = ortho_ref[pl.ds(pl.multiple_of(row + step * rows, 16), rows), :]
        approx = dot(left, stack_ref[:, col : col + cols], (1, 0))
        residue[0] = merged[which][here, :] - approx
        speed = MOMENTUM_DECAY * moments[which][here, :] + approx
        velocity[...] = speed
        master[...] = weights[which][here, :] - LEARN_RATE * speed


def per_device(sizes, *arrays):
    weight_in, weight_out, query_in = arrays[2], arrays[7], arrays[4]
    replicas, shards, tensors = sizes
    rows_in, cols_in = weight_in.shape
    rows_out, cols_out = weight_out.shape
    rank = query_in.shape[1]
    row_at, col_at = up(rows_out, LANES), up(cols_out, LANES)
    left_axes = (("replica", "tensor"), (replicas, tensors), rank)
    left_out, left_in = Group(*left_axes, rows_out), Group(*left_axes, rows_in)
    right = Group(("replica", "shard"), (replicas, shards), rank, col_at + cols_in + 2 * rank)
    gram = Group(("shard",), (shards,), rank, LANES)
    groups = (left_out, left_in, right, gram)
    vmem = pl.BlockSpec(memory_space=pltpu.VMEM)
    packed = up(4 * rank, LANES)

    def room(group):
        return [
            pltpu.VMEM((ROUNDS, rank, group.total), F32),
            pltpu.VMEM((ROUNDS, group.slots(), group.rows, group.width), F32),
            pltpu.VMEM((ROUNDS, rank, group.total), F32),
            pltpu.SemaphoreType.DMA((ROUNDS, 4, group.slots())),
        ]

    both = (weight_in.shape, weight_out.shape)
    operands = [array.T if array.shape[-1] == rank else array for array in arrays]
    operands = [pltpu.with_memory_space_constraint(array, pltpu.HBM) for array in operands]
    carried = pl.pallas_call(
        functools.partial(factors_kernel, groups, replicas),
        out_shape=(
            *[jax.ShapeDtypeStruct(shape, F32) for shape in both * 3],
            jax.ShapeDtypeStruct((row_at + up(rows_in, LANES), 3 * rank), BF16),
            jax.ShapeDtypeStruct((3 * rank, col_at + up(cols_in, LANES)), BF16),
            jax.ShapeDtypeStruct((rank, cols_in), F32),
            jax.ShapeDtypeStruct((rank, cols_out), F32),
        ),
        in_specs=[pl.BlockSpec(memory_space=pltpu.HBM)] * 10,
        out_specs=(vmem,) * 10,
        scratch_shapes=[
            *[pltpu.VMEM((1, *shape), BF16) for shape in both],
            *[pltpu.VMEM((1, *shape), F32) for shape in both],
            *[pltpu.VMEM((rank, shape[1]), F32) for shape in both],
            *[pltpu.VMEM(shape, BF16) for shape in both * 2],
            pltpu.SemaphoreType.DMA((10,)),
            *[space for group in groups[:3] for space in room(group)],
            pltpu.VMEM((ROUNDS, rank // 2, packed), F32),
            pltpu.VMEM((ROUNDS, gram.slots(), rank // 2, packed), F32),
            pltpu.VMEM((ROUNDS, 8, packed), F32),
            pltpu.SemaphoreType.DMA((ROUNDS, 2, gram.slots())),
        ],
        compiler_params=pltpu.CompilerParams(collective_id=0, has_side_effects=True, vmem_limit_bytes=24 << 20),
        name="factors",
    )(*operands)

    steps = math.gcd(rows_in // 16, rows_out // 16, 4)

    def rows_of(shape):
        return pl.BlockSpec((shape[0] // steps, shape[1]), lambda step: (step, 0))

    def cube_of(shape):
        return pl.BlockSpec((1, shape[0] // steps, shape[1]), lambda step: (0, step, 0))

    results, specs = [], []
    for shape in both:
        results += [shape, shape, (1, *shape), (rank, shape[1])]
        specs += [rows_of(shape), rows_of(shape), cube_of(shape), pl.BlockSpec((rank, shape[1]), lambda step: (0, 0))]
    finished = pl.pallas_call(
        functools.partial(finish_kernel, (row_at, col_at)),
        grid=(steps,),
        out_shape=tuple(jax.ShapeDtypeStruct(shape, F32) for shape in results),
        in_specs=[vmem] * 10,
        out_specs=tuple(specs),
        compiler_params=pltpu.CompilerParams(vmem_limit_bytes=24 << 20),
        name="finish",
    )(*carried)
    return tuple(array.T if place % 4 == 3 else array for place, array in enumerate(finished))


def solution(mesh):
    sizes = (mesh.shape["replica"], mesh.shape["shard"], mesh.shape["tensor"])
    cube, flat, thin = P("replica", "shard", "tensor"), P("shard", "tensor"), P("tensor", None)
    return jax.shard_map(
        functools.partial(per_device, sizes),
        mesh=mesh,
        in_specs=(cube, cube, flat, flat, thin) * 2,
        out_specs=(flat, flat, cube, thin) * 2,
        check_vma=False,
    )
```
